32 devices in a mesh: blk: 4 (over z), rep: 8 (over y, x, core).
Axes of the slice: x: 2, y: 2, z: 4, core: 2. Of those that a mesh axis runs over, the one named last changes fastest.
Arguments:
- photo_features: bfloat16 [8, 2048, 1152], P('rep', 'blk'), may hold values from -6 to 6
- wording_features: bfloat16 [8, 2048, 1152], P('rep', 'blk'), may hold values from -6 to 6
- partner_wording_slot: int32 [8, 2048], P('rep', 'blk'), may hold values from 0 to 2047, each once within a row
- photo_projector_weights: bfloat16 [1152, 1152], replicated, may hold values from -0.1875 to 0.1875
- wording_projector_weights: bfloat16 [1152, 1152], replicated, may hold values from -0.1875 to 0.1875
- learned_inverse_heat: float32 [1], replicated, may hold values from 4 to 12
- offset_term: float32 [1], replicated, may hold values from -3 to -1
Outputs:
- grad_img_head: float32 [1152, 1152], replicated
- grad_txt_head: float32 [1152, 1152], replicated
The draws below stay inside these ranges and needn't reach their ends.
Inputs may be any that keep to these rules, and one draw needn't show every extreme that they name: `partner_wording_slot`: within each group the 2048 images name distinct texts of that group.
All inputs are finite; a program needn't handle non-finite values.
Results may differ from the reference program's by a relative error of at most 0.0029.
Values may be sent and summed in bfloat16 or wider, within the bound.
A program may use at most 128 MiB of HBM per device.

```python
import jax
import jax.numpy as jnp
from jax import lax

WIDTH = 1152
EMBED = 1152
ROWS_DEV = 512
STEPS = 4
GROUP_ROWS = 2048
N_BLK = 4
N_REP = 8


def block_scale(stream_key, shape, cuts, least, high):
    gain, own = 1.0, jax.random.fold_in(stream_key, 6)
    for axis_at, shards_of in cuts:
        heights = jnp.exp(jax.random.uniform(jax.random.fold_in(own, axis_at), (shards_of,), jnp.float32, least / len(cuts), high / len(cuts)))
        gain = gain * jnp.repeat(heights, shape[axis_at] // shards_of).reshape([-1 if axis == axis_at else 1 for axis in range(len(shape))])
    return gain


def centred(rng, extent, deviation, limit, pieces=(), kind=jnp.bfloat16):
    array = deviation * jax.random.normal(rng, extent, jnp.float32)
    if pieces:
        array = array * block_scale(rng, extent, pieces, -0.22, 0.18)
    return jnp.clip(array, -limit, limit).astype(kind)


def setup_inputs(seed: int = 0) -> dict:
    streams_of = jax.random.split(jax.random.key(seed), 8)
    return {
        "photo_features": centred(streams_of[0], (N_REP, GROUP_ROWS, WIDTH), 1.0, 6.0, ((0, 8), (1, 4))),
        "wording_features": centred(streams_of[1], (N_REP, GROUP_ROWS, WIDTH), 1.0, 6.0, ((0, 8), (1, 4))),
        "partner_wording_slot": jax.vmap(lambda own: jax.random.permutation(own, GROUP_ROWS))(jax.random.split(streams_of[2], N_REP)).reshape((N_REP, GROUP_ROWS)).astype(jnp.int32),
        "photo_projector_weights": centred(streams_of[3], (WIDTH, EMBED), WIDTH ** -0.5, 0.1875),
        "wording_projector_weights": centred(streams_of[4], (WIDTH, EMBED), WIDTH ** -0.5, 0.1875),
        "learned_inverse_heat": jnp.clip(jax.random.uniform(streams_of[5], (1,), jnp.float32, 4.0, 12.0), 4.0, 12.0),
        "offset_term": jnp.clip(jax.random.uniform(streams_of[6], (1,), jnp.float32, -3.0, -1.0), -3.0, -1.0),
    }


epsilon = 1e-06
criterion_prefactor = 0.0625

def normalize(features, head):
    projected = jnp.dot(features, head, preferred_element_type=jnp.float32)
    inverse = lax.rsqrt(lax.optimization_barrier(jnp.sum(projected * projected, axis=-1, keepdims=True)) + epsilon)
    unit = projected * inverse
    return (unit, unit.astype(jnp.bfloat16), inverse)

def unnormalize(unit, inverse, upstream):
    inner = lax.optimization_barrier(jnp.sum(unit * upstream, axis=-1, keepdims=True))
    return (inverse * (upstream - unit * inner)).astype(jnp.bfloat16)

def reference(photo_features, wording_features, partner_wording_slot, photo_projector_weights, wording_projector_weights, learned_inverse_heat, offset_term):
    positions = jnp.arange(GROUP_ROWS, dtype=jnp.int32)
    panel_of = positions // ROWS_DEV
    diagonal_band_span = (panel_of[:, None] - panel_of[None, :]) % N_BLK < STEPS
    exponentiated_heat = learned_inverse_heat[0] * criterion_prefactor

    def one_group(totals, group):
        image_rows, text_rows, targets = group
        img_unit, img_low, img_inv = normalize(image_rows, photo_projector_weights)
        txt_unit, txt_low, txt_inv = normalize(text_rows, wording_projector_weights)
        cosine_agreement_table = jnp.dot(img_low, txt_low.T, preferred_element_type=jnp.float32)
        unbounded_pairwise_array = learned_inverse_heat[0] * cosine_agreement_table + offset_term[0]
        diagonal_label = (targets[:, None] == positions[None, :]).astype(jnp.float32)
        sigmoid_error = jnp.where(diagonal_band_span, exponentiated_heat * (jax.nn.sigmoid(unbounded_pairwise_array) - diagonal_label), 0.0).astype(jnp.bfloat16)
        d_img = jnp.dot(sigmoid_error, txt_low, preferred_element_type=jnp.float32)
        d_txt = jnp.dot(sigmoid_error.T, img_low, preferred_element_type=jnp.float32)
        grad_img = jnp.dot(image_rows.T, unnormalize(img_unit, img_inv, d_img), preferred_element_type=jnp.float32)
        grad_txt = jnp.dot(text_rows.T, unnormalize(txt_unit, txt_inv, d_txt), preferred_element_type=jnp.float32)
        return ((totals[0] + grad_img, totals[1] + grad_txt), None)
    zeros = jnp.zeros((WIDTH, EMBED), jnp.float32)
    totals, unused = lax.scan(one_group, (zeros, zeros), (photo_features, wording_features, partner_wording_slot))
    return (totals[0], totals[1])
```

```python
import functools

import jax
import jax.numpy as jnp
from jax import lax
from jax.experimental import pallas as pl
from jax.experimental.pallas import tpu as pltpu
from jax.sharding import PartitionSpec as P

STEPS = 4
MESH = pl.DeviceIdType.MESH
CHUNKS = 3
PAD = 16


epsilon = 1e-06
criterion_prefactor = 0.0625


def from_behind(array, axis, by):
    count = lax.axis_size(axis)
    return lax.ppermute(array, axis, [(i, (i + by) % count) for i in range(count)])


def normalize(features, head):
    projected = jnp.dot(features, head, preferred_element_type=jnp.float32)
    inverse = lax.rsqrt(jnp.sum(projected * projected, axis=-1, keepdims=True) + epsilon)
    unit = projected * inverse
    return (unit, unit.astype(jnp.bfloat16), inverse)


def unnormalize(unit, inverse, upstream):
    inner = jnp.sum(unit * upstream, axis=-1, keepdims=True)
    return (inverse * (upstream - unit * inner)).astype(jnp.bfloat16)


def across_rows(left, right):
    return lax.dot_general(
        left, right, (((0,), (0,)), ((), ())), preferred_element_type=jnp.float32
    )


def ring_local(
    photo_features,
    wording_features,
    partner_wording_slot,
    photo_projector_weights,
    wording_projector_weights,
    learned_inverse_heat,
    offset_term,
):
    image_rows = photo_features[0]
    text_rows = wording_features[0]
    targets = partner_wording_slot[0]
    row_count = image_rows.shape[0]
    block_count = lax.axis_size("blk")
    position = lax.axis_index("blk")
    img_unit, img_low, img_inv = normalize(image_rows, photo_projector_weights)
    txt_unit, txt_low, txt_inv = normalize(text_rows, wording_projector_weights)
    exponentiated_heat = learned_inverse_heat[0] * criterion_prefactor
    offsets = jnp.arange(row_count, dtype=jnp.int32)
    d_img = jnp.zeros((row_count, txt_low.shape[1]), jnp.float32)
    panel = txt_low
    partial_value = jnp.zeros((row_count, txt_low.shape[1]), jnp.float32)
    for step_index in range(STEPS):
        if step_index > 0:
            panel = from_behind(panel, "blk", 1)
            partial_value = from_behind(partial_value, "blk", 1)
        cosine_agreement_table = lax.dot_general(
            img_low, panel, (((1,), (1,)), ((), ())), preferred_element_type=jnp.float32
        )
        unbounded_pairwise_array = learned_inverse_heat[0] * cosine_agreement_table + offset_term[0]
        columns = (position - step_index) % block_count * row_count + offsets
        diagonal_label = (targets[:, None] == columns[None, :]).astype(jnp.float32)
        submatrix_block_piece = (
            exponentiated_heat * (jax.nn.sigmoid(unbounded_pairwise_array) - diagonal_label)
        ).astype(jnp.bfloat16)
        d_img = d_img + jnp.dot(submatrix_block_piece, panel, preferred_element_type=jnp.float32)
        partial_value = partial_value + across_rows(submatrix_block_piece, img_low)
    d_txt = from_behind(partial_value, "blk", -(STEPS - 1))
    grad_img = across_rows(image_rows, unnormalize(img_unit, img_inv, d_img))
    grad_txt = across_rows(text_rows, unnormalize(txt_unit, txt_inv, d_txt))
    grad_img, grad_txt = lax.psum((grad_img, grad_txt), ("blk", "rep"))
    return (grad_img, grad_txt)


def reduce_kernel(
    n_z, img_ref, txt_ref, out_ref, got0, acc, s1, r1, s2, r2, r3, send, recv
):
    rows, cols = img_ref.shape
    width = cols // CHUNKS
    half, quarter = rows // 2, rows // 4
    piece = quarter // n_z
    padded = out_ref.shape[4]
    z, r = lax.axis_index("blk"), lax.axis_index("rep")
    core, x, y = r % 2, (r // 2) % 2, r // 4
    a1 = x + core * (y - x)
    a2 = y + core * (x - y)
    sibling = r + 1 - 2 * core
    p1 = r + (2 + 2 * core) * (1 - 2 * a1)
    p2 = r + (4 - 2 * core) * (1 - 2 * a2)
    turn = [lax.rem(z + d, n_z) for d in range(n_z)]
    back = [lax.rem(z - d + n_z, n_z) for d in range(n_z)]

    barrier = pltpu.get_barrier_semaphore()
    for who in [(z, sibling), (z, p1), (z, p2)] + [(turn[d], r) for d in range(1, n_z)]:
        pl.semaphore_signal(barrier, inc=1, device_id=who, device_id_type=MESH)
    pl.semaphore_wait(barrier, 2 + n_z)

    def span(c):
        return pl.ds(c * width, width)

    def copy(src, dst, c, slot, who):
        return pltpu.make_async_remote_copy(
            src_ref=src,
            dst_ref=dst,
            send_sem=send.at[c, slot],
            recv_sem=recv.at[c, slot],
            device_id=who,
            device_id_type=MESH,
        )

    def of(start, size, step):
        return pl.ds(pl.multiple_of(start, step), size)

    keep1 = of(a1 * half, half, 16)
    give1 = of((1 - a1) * half, half, 16)
    base2 = a1 * half + a2 * quarter
    keep2 = of(base2, quarter, 8)
    give2 = of(a1 * half + (1 - a2) * quarter, quarter, 8)
    mine2 = of(a2 * quarter, quarter, 8)

    def c0(c, ref):
        return copy(ref.at[:, span(c)], got0.at[:, span(c)], c, 0, (z, sibling))

    def c1(c):
        return copy(s1.at[:, span(c)], r1.at[:, span(c)], c, 1, (z, p1))

    def c2(c):
        return copy(s2.at[:, span(c)], r2.at[:, span(c)], c, 2, (z, p2))

    def c3(c, d):
        src = acc.at[of(base2 + turn[d] * piece, piece, 8), span(c)]
        return copy(src, r3.at[d, :, span(c)], c, 2 + d, (turn[d], r))

    def g3(c, d):
        slot = out_ref.at[core, a1, a2, z, :, span(c)]
        return copy(slot, slot, c, 1 + n_z + d, (turn[d], r))

    def g3_in(c, d):
        slot = out_ref.at[core, a1, a2, back[d], :, span(c)]
        return copy(slot, slot, c, 1 + n_z + d, (turn[d], r))

    def g2(c, part):
        slot = out_ref.at[core, a1, part, :, :, span(c)]
        return copy(slot, slot, c, 1 + 2 * n_z, (z, p2))

    def g1(c, part):
        slot = out_ref.at[core, part, :, :, :, span(c)]
        return copy(slot, slot, c, 2 + 2 * n_z, (z, p1))

    def g0(c, part):
        slot = out_ref.at[part, :, :, :, :, span(c)]
        return copy(slot, slot, c, 3 + 2 * n_z, (z, sibling))

    def stage0(c):
        @pl.when(core == 0)
        def _():
            c0(c, txt_ref).start()

        @pl.when(core == 1)
        def _():
            c0(c, img_ref).start()

    def stage1(c):
        c0(c, img_ref).wait()

        def add(ref):
            s1[:, span(c)] = (ref[give1, span(c)] + got0[give1, span(c)]).astype(s1.dtype)
            c1(c).start()
            acc[keep1, span(c)] = ref[keep1, span(c)] + got0[keep1, span(c)]

        @pl.when(core == 0)
        def _():
            add(img_ref)

        @pl.when(core == 1)
        def _():
            add(txt_ref)

    def stage2(c):
        c1(c).wait()
        other2 = of((1 - a2) * quarter, quarter, 16)
        s2[:, span(c)] = (acc[give2, span(c)] + r1[other2, span(c)].astype(jnp.float32)).astype(s2.dtype)
        c2(c).start()
        own2 = of(a2 * quarter, quarter, 16)
        acc[keep2, span(c)] = acc[keep2, span(c)] + r1[own2, span(c)].astype(jnp.float32)

    def stage3(c):
        c2(c).wait()
        acc[keep2, span(c)] = acc[keep2, span(c)] + r2[:, span(c)].astype(jnp.float32)
        for d in range(1, n_z):
            c3(c, d).start()

    def stage4(c):
        total = acc[of(base2 + z * piece, piece, 8), span(c)]
        for d in range(1, n_z):
            c3(c, d).wait()
            total = total + r3[d, :, span(c)]
        if padded > piece:
            total = jnp.concatenate([total, jnp.zeros((padded - piece, width), jnp.float32)], axis=0)
        out_ref[core, a1, a2, z, :, span(c)] = total.astype(out_ref.dtype)
        for d in range(1, n_z):
            g3(c, d).start()

    def stage5(c):
        for d in range(1, n_z):
            g3_in(c, d).wait_recv()
        g2(c, a2).start()

    def stage6(c):
        g2(c, 1 - a2).wait_recv()
        g1(c, a1).start()

    def stage7(c):
        g1(c, 1 - a1).wait_recv()
        g0(c, core).start()

    def stage8(c):
        g0(c, 1 - core).wait_recv()
        for d in range(1, n_z):
            g3(c, d).wait_send()
        g2(c, a2).wait_send()
        g1(c, a1).wait_send()
        g0(c, core).wait_send()

    for c in range(CHUNKS):
        stage0(c)
    stages = [stage1, stage2, stage3, stage4, stage5, stage6, stage7, stage8]
    for tick in range(CHUNKS + len(stages) - 1):
        for at in range(len(stages)):
            if 0 <= tick - at < CHUNKS:
                stages[at](tick - at)


def reduce_all(grad_img, grad_txt, n_z):
    rows, cols = grad_img.shape
    half, quarter = rows // 2, rows // 4
    piece = quarter // n_z
    padded = -(-piece // PAD) * PAD
    low = jnp.bfloat16
    out = pl.pallas_call(
        functools.partial(reduce_kernel, n_z),
        out_shape=jax.ShapeDtypeStruct((2, 2, 2, n_z, padded, cols), low),
        in_specs=[pl.BlockSpec(memory_space=pltpu.VMEM)] * 2,
        out_specs=pl.BlockSpec(memory_space=pltpu.VMEM),
        scratch_shapes=[
            pltpu.VMEM((rows, cols), jnp.float32),
            pltpu.VMEM((rows, cols), jnp.float32),
            pltpu.VMEM((half, cols), low),
            pltpu.VMEM((half, cols), low),
            pltpu.VMEM((quarter, cols), low),
            pltpu.VMEM((quarter, cols), low),
            pltpu.VMEM((n_z, piece, cols), jnp.float32),
            pltpu.SemaphoreType.DMA((CHUNKS, 4 + 2 * n_z)),
            pltpu.SemaphoreType.DMA((CHUNKS, 4 + 2 * n_z)),
        ],
        compiler_params=pltpu.CompilerParams(
            collective_id=0, has_side_effects=True, vmem_limit_bytes=50 * 1024 * 1024
        ),
        cost_estimate=pl.CostEstimate(flops=10**9, bytes_accessed=10**8, transcendentals=0),
    )(grad_img, grad_txt)
    by_core = [out[c, :, :, :, :piece].astype(jnp.float32) for c in range(2)]
    return tuple(part.reshape(rows, cols) for part in by_core)


def tile_local(
    photo_features,
    wording_features,
    partner_wording_slot,
    photo_projector_weights,
    wording_projector_weights,
    learned_inverse_heat,
    offset_term,
):
    position = lax.axis_index("blk")
    row_count = photo_features.shape[1]
    swap1 = [(i, i ^ 1) for i in range(4)]
    swap2 = [(i, i ^ 2) for i in range(4)]
    photos = [photo_features[0], lax.ppermute(photo_features[0], "blk", swap1)]
    wordings = [wording_features[0], lax.ppermute(wording_features[0], "blk", swap2)]
    targets = [partner_wording_slot[0], lax.ppermute(partner_wording_slot[0], "blk", swap1)]
    text_block = [position, (position + 2) % 4]
    heat, offset = learned_inverse_heat[0], offset_term[0]
    offsets = jnp.arange(row_count, dtype=jnp.int32)
    images = [normalize(rows, photo_projector_weights) for rows in photos]
    texts = [normalize(rows, wording_projector_weights) for rows in wordings]

    def resid(a, b):
        cosine = lax.dot_general(
            images[a][1], texts[b][1], (((1,), (1,)), ((), ())), preferred_element_type=jnp.float32
        )
        label = (targets[a][:, None] == (text_block[b] * row_count + offsets)[None, :]).astype(jnp.float32)
        return (heat * criterion_prefactor * (jax.nn.sigmoid(heat * cosine + offset) - label)).astype(jnp.bfloat16)

    pieces = [[resid(a, b) for b in range(2)] for a in range(2)]

    def grad_of(rows, own, upstream):
        return sum(
            across_rows(rows[k], unnormalize(own[k][0], own[k][2], upstream[k])) for k in range(2)
        )

    d_img = [
        sum(jnp.dot(pieces[a][b], texts[b][1], preferred_element_type=jnp.float32) for b in range(2))
        for a in range(2)
    ]
    d_txt = [sum(across_rows(pieces[a][b], images[a][1]) for a in range(2)) for b in range(2)]
    grad_img = grad_of(photos, images, d_img)
    grad_txt = grad_of(wordings, texts, d_txt)
    return reduce_all(grad_img, grad_txt, 4)


def solution(mesh):
    placed = (P("rep", "blk", None), P("rep", "blk", None), P("rep", "blk"), P(), P(), P(), P())
    tiled = mesh.shape["blk"] == STEPS == 4 and mesh.shape["rep"] == 8
    body = tile_local if tiled else ring_local
    return jax.shard_map(body, mesh=mesh, in_specs=placed, out_specs=(P(), P()), check_vma=False)
```

```python
import functools

import jax
import jax.numpy as jnp
from jax import lax
from jax.experimental import pallas as pl
from jax.experimental.pallas import tpu as pltpu
from jax.sharding import PartitionSpec as P

STEPS = 4
MESH = pl.DeviceIdType.MESH
WIDTH = 128
PAD = 16


epsilon = 1e-06
criterion_prefactor = 0.0625


def from_behind(array, axis, by):
    count = lax.axis_size(axis)
    return lax.ppermute(array, axis, [(i, (i + by) % count) for i in range(count)])


def normalize(features, head):
    projected = jnp.dot(features, head, preferred_element_type=jnp.float32)
    inverse = lax.rsqrt(jnp.sum(projected * projected, axis=-1, keepdims=True) + epsilon)
    unit = projected * inverse
    return (unit, unit.astype(jnp.bfloat16), inverse)


def unnormalize(unit, inverse, upstream):
    inner = jnp.sum(unit * upstream, axis=-1, keepdims=True)
    return (inverse * (upstream - unit * inner)).astype(jnp.bfloat16)


def across_rows(left, right):
    return lax.dot_general(
        left, right, (((0,), (0,)), ((), ())), preferred_element_type=jnp.float32
    )


def ring_local(
    photo_features,
    wording_features,
    partner_wording_slot,
    photo_projector_weights,
    wording_projector_weights,
    learned_inverse_heat,
    offset_term,
):
    image_rows = photo_features[0]
    text_rows = wording_features[0]
    targets = partner_wording_slot[0]
    row_count = image_rows.shape[0]
    block_count = lax.axis_size("blk")
    position = lax.axis_index("blk")
    img_unit, img_low, img_inv = normalize(image_rows, photo_projector_weights)
    txt_unit, txt_low, txt_inv = normalize(text_rows, wording_projector_weights)
    exponentiated_heat = learned_inverse_heat[0] * criterion_prefactor
    offsets = jnp.arange(row_count, dtype=jnp.int32)
    d_img = jnp.zeros((row_count, txt_low.shape[1]), jnp.float32)
    panel = txt_low
    partial_value = jnp.zeros((row_count, txt_low.shape[1]), jnp.float32)
    for step_index in range(STEPS):
        if step_index > 0:
            panel = from_behind(panel, "blk", 1)
            partial_value = from_behind(partial_value, "blk", 1)
        cosine_agreement_table = lax.dot_general(
            img_low, panel, (((1,), (1,)), ((), ())), preferred_element_type=jnp.float32
        )
        unbounded_pairwise_array = learned_inverse_heat[0] * cosine_agreement_table + offset_term[0]
        columns = (position - step_index) % block_count * row_count + offsets
        diagonal_label = (targets[:, None] == columns[None, :]).astype(jnp.float32)
        submatrix_block_piece = (
            exponentiated_heat * (jax.nn.sigmoid(unbounded_pairwise_array) - diagonal_label)
        ).astype(jnp.bfloat16)
        d_img = d_img + jnp.dot(submatrix_block_piece, panel, preferred_element_type=jnp.float32)
        partial_value = partial_value + across_rows(submatrix_block_piece, img_low)
    d_txt = from_behind(partial_value, "blk", -(STEPS - 1))
    grad_img = across_rows(image_rows, unnormalize(img_unit, img_inv, d_img))
    grad_txt = across_rows(text_rows, unnormalize(txt_unit, txt_inv, d_txt))
    grad_img, grad_txt = lax.psum((grad_img, grad_txt), ("blk", "rep"))
    return (grad_img, grad_txt)


def reduce_kernel(
    n_z, xi0, xi1, xt0, xt1, di0, di1, dt0, dt1, img_ref, txt_ref,
    give, got0, acc, s1, r1, r2, r3, pool, send, recv
):
    rows, cols = img_ref.shape
    chunks, _, width = acc.shape
    panels, _, wide = give.shape
    per = chunks // panels
    half, quarter = rows // 2, rows // 4
    piece = quarter // n_z
    padded = pool.shape[5]
    z, r = lax.axis_index("blk"), lax.axis_index("rep")
    core, x, y = r % 2, (r // 2) % 2, r // 4
    a1 = x + core * (y - x)
    a2 = y + core * (x - y)
    sibling = r + 1 - 2 * core
    p1 = r + (2 + 2 * core) * (1 - 2 * a1)
    p2 = r + (4 - 2 * core) * (1 - 2 * a2)
    turn = [lax.rem(z + d, n_z) for d in range(n_z)]
    back = [lax.rem(z - d + n_z, n_z) for d in range(n_z)]

    barrier = pltpu.get_barrier_semaphore()
    for who in [(z, sibling), (z, p1), (z, p2)] + [(turn[d], r) for d in range(1, n_z)]:
        pl.semaphore_signal(barrier, inc=1, device_id=who, device_id_type=MESH)
    pl.semaphore_wait(barrier, 2 + n_z)

    def copy(src, dst, c, slot, who):
        return pltpu.make_async_remote_copy(
            src_ref=src,
            dst_ref=dst,
            send_sem=send.at[c, slot],
            recv_sem=recv.at[c, slot],
            device_id=who,
            device_id_type=MESH,
        )

    def of(start, size, step):
        return pl.ds(pl.multiple_of(start, step), size)

    keep1 = of(a1 * half, half, 16)
    give1 = of((1 - a1) * half, half, 16)
    base2 = a1 * half + a2 * quarter
    keep2 = of(base2, quarter, 8)
    give2 = of(a1 * half + (1 - a2) * quarter, quarter, 8)
    own2 = of(a2 * quarter, quarter, 16)
    other2 = of((1 - a2) * quarter, quarter, 16)

    def c0(m):
        return copy(give.at[m], got0.at[m], m, 0, (z, sibling))

    def c1(c):
        return copy(s1.at[c], r1.at[c], c, 1, (z, p1))

    def c2(c):
        return copy(acc.at[c, give2], r2.at[c], c, 2, (z, p2))

    def c3(c, d):
        src = acc.at[c, of(base2 + turn[d] * piece, piece, 8)]
        return copy(src, r3.at[c, d], c, 2 + d, (turn[d], r))

    def g3(c, d, at):
        slot = pool.at[c, core, a1, a2, at]
        return copy(slot, slot, c, 1 + n_z + d, (turn[d], r))

    def g2(c, part):
        slot = pool.at[c, core, a1, part]
        return copy(slot, slot, c, 1 + 2 * n_z, (z, p2))

    def g1(c, part):
        slot = pool.at[c, core, part]
        return copy(slot, slot, c, 2 + 2 * n_z, (z, p1))

    def g0(c, part):
        slot = pool.at[c, part]
        return copy(slot, slot, c, 3 + 2 * n_z, (z, sibling))

    tile = rows // 3

    def product(left, right, m, store):
        columns = pl.ds(m * wide, wide)

        def body(i, carry):
            at = pl.ds(pl.multiple_of(i * tile, tile), tile)
            store(
                at,
                jnp.dot(left[0][at, :], right[0][:, columns], preferred_element_type=jnp.float32)
                + jnp.dot(left[1][at, :], right[1][:, columns], preferred_element_type=jnp.float32),
            )
            return carry

        lax.fori_loop(0, rows // tile, body, 0)

    def of_head(head, m, store):
        if head == 0:
            product((xi0, xi1), (di0, di1), m, store)
        else:
            product((xt0, xt1), (dt0, dt1), m, store)

    def theirs(m):
        def store(at, value):
            give[m, at, :] = value

        for mine in range(2):
            @pl.when(core == mine)
            def _():
                of_head(1 - mine, m, store)

        c0(m).start()

    def ours(m):
        def store(at, value):
            for j in range(per):
                acc[m * per + j, at, :] = value[:, j * width : (j + 1) * width]

        for mine in range(2):
            @pl.when(core == mine)
            def _():
                of_head(mine, m, store)

    def stage1(c):
        m, part = c // per, pl.ds(c % per * width, width)
        if c % per == 0:
            c0(m).wait()
        s1[c] = (acc[c, give1, :] + got0[m, give1, part]).astype(s1.dtype)
        c1(c).start()
        acc[c, keep1, :] = acc[c, keep1, :] + got0[m, keep1, part]

    def stage2(c):
        c1(c).wait()
        acc[c, give2, :] = acc[c, give2, :] + r1[c, other2, :].astype(jnp.float32)
        c2(c).start()
        acc[c, keep2, :] = acc[c, keep2, :] + r1[c, own2, :].astype(jnp.float32)

    def stage3(c):
        c2(c).wait()
        acc[c, keep2, :] = acc[c, keep2, :] + r2[c]
        for d in range(1, n_z):
            c3(c, d).start()

    def stage4(c):
        total = acc[c, of(base2 + z * piece, piece, 8), :]
        for d in range(1, n_z):
            c3(c, d).wait()
            total = total + r3[c, d]
        if padded > piece:
            total = jnp.concatenate([total, jnp.zeros((padded - piece, width), jnp.float32)], axis=0)
        pool[c, core, a1, a2, z] = total.astype(pool.dtype)
        for d in range(1, n_z):
            g3(c, d, z).start()

    def stage5(c):
        for d in range(1, n_z):
            g3(c, d, back[d]).wait_recv()
        g2(c, a2).start()

    def stage6(c):
        g2(c, 1 - a2).wait_recv()
        g1(c, a1).start()

    def stage7(c):
        g1(c, 1 - a1).wait_recv()
        g0(c, core).start()

    def stage8(c):
        g0(c, 1 - core).wait_recv()
        for head, ref in ((0, img_ref), (1, txt_ref)):
            for k in range(4 * n_z):
                value = pool[c, head, k // (2 * n_z), k // n_z % 2, k % n_z].astype(jnp.float32)
                ref[k * piece : (k + 1) * piece, c * width : (c + 1) * width] = value[:piece]
        for d in range(1, n_z):
            g3(c, d, z).wait_send()
        g2(c, a2).wait_send()
        g1(c, a1).wait_send()
        g0(c, core).wait_send()

    for m in range(panels):
        theirs(m)
    stages = [stage1, stage2, stage3, stage4, stage5, stage6, stage7, stage8]
    for tick in range(chunks + len(stages) - 1):
        if tick < chunks and tick % per == 0:
            ours(tick // per)
        for at in range(len(stages)):
            if 0 <= tick - at < chunks:
                stages[at](tick - at)


def reduce_all(operands, n_z):
    rows, cols = operands[0].shape[0], operands[4].shape[1]
    half, quarter = rows // 2, rows // 4
    piece = quarter // n_z
    padded = -(-piece // PAD) * PAD
    chunks, width = cols // WIDTH, WIDTH
    panels = chunks // 3
    low, full = jnp.bfloat16, jnp.float32
    return pl.pallas_call(
        functools.partial(reduce_kernel, n_z),
        out_shape=[jax.ShapeDtypeStruct((rows, cols), full)] * 2,
        in_specs=[pl.BlockSpec(memory_space=pltpu.VMEM)] * 8,
        out_specs=[pl.BlockSpec(memory_space=pltpu.VMEM)] * 2,
        scratch_shapes=[
            pltpu.VMEM((panels, rows, 3 * width), full),
            pltpu.VMEM((panels, rows, 3 * width), full),
            pltpu.VMEM((chunks, rows, width), full),
            pltpu.VMEM((chunks, half, width), low),
            pltpu.VMEM((chunks, half, width), low),
            pltpu.VMEM((chunks, quarter, width), full),
            pltpu.VMEM((chunks, n_z, piece, width), full),
            pltpu.VMEM((chunks, 2, 2, 2, n_z, padded, width), low),
            pltpu.SemaphoreType.DMA((chunks, 4 + 2 * n_z)),
            pltpu.SemaphoreType.DMA((chunks, 4 + 2 * n_z)),
        ],
        compiler_params=pltpu.CompilerParams(
            collective_id=0, has_side_effects=True, vmem_limit_bytes=58 * 1024 * 1024
        ),
        cost_estimate=pl.CostEstimate(flops=6 * 10**9, bytes_accessed=10**8, transcendentals=0),
    )(*operands)


def tile_local(
    photo_features,
    wording_features,
    partner_wording_slot,
    photo_projector_weights,
    wording_projector_weights,
    learned_inverse_heat,
    offset_term,
):
    position = lax.axis_index("blk")
    row_count = photo_features.shape[1]
    swap1 = [(i, i ^ 1) for i in range(4)]
    swap2 = [(i, i ^ 2) for i in range(4)]
    photos = [photo_features[0], lax.ppermute(photo_features[0], "blk", swap1)]
    wordings = [wording_features[0], lax.ppermute(wording_features[0], "blk", swap2)]
    targets = [partner_wording_slot[0], lax.ppermute(partner_wording_slot[0], "blk", swap1)]
    text_block = [position, (position + 2) % 4]
    heat, offset = learned_inverse_heat[0], offset_term[0]
    offsets = jnp.arange(row_count, dtype=jnp.int32)
    images = [normalize(rows, photo_projector_weights) for rows in photos]
    texts = [normalize(rows, wording_projector_weights) for rows in wordings]

    def resid(a, b):
        cosine = lax.dot_general(
            images[a][1], texts[b][1], (((1,), (1,)), ((), ())), preferred_element_type=jnp.float32
        )
        label = (targets[a][:, None] == (text_block[b] * row_count + offsets)[None, :]).astype(jnp.float32)
        return (heat * criterion_prefactor * (jax.nn.sigmoid(heat * cosine + offset) - label)).astype(jnp.bfloat16)

    pieces = [[resid(a, b) for b in range(2)] for a in range(2)]

    d_img = [
        sum(jnp.dot(pieces[a][b], texts[b][1], preferred_element_type=jnp.float32) for b in range(2))
        for a in range(2)
    ]
    d_txt = [sum(across_rows(pieces[a][b], images[a][1]) for a in range(2)) for b in range(2)]
    lefts = [rows.T for rows in photos + wordings]
    rights = [unnormalize(own[0], own[2], up) for own, up in zip(images + texts, d_img + d_txt)]
    return tuple(reduce_all(lefts + rights, 4))


def solution(mesh):
    placed = (P("rep", "blk", None), P("rep", "blk", None), P("rep", "blk"), P(), P(), P(), P())
    tiled = mesh.shape["blk"] == STEPS == 4 and mesh.shape["rep"] == 8
    body = tile_local if tiled else ring_local
    return jax.shard_map(body, mesh=mesh, in_specs=placed, out_specs=(P(), P()), check_vma=False)
```

```python
import functools

import jax
import jax.numpy as jnp
from jax import lax
from jax.experimental import pallas as pl
from jax.experimental.pallas import tpu as pltpu
from jax.sharding import PartitionSpec as P

STEPS = 4
MESH = pl.DeviceIdType.MESH
WIDTH = 128
PAD = 16


epsilon = 1e-06
criterion_prefactor = 0.0625


def from_behind(array, axis, by):
    count = lax.axis_size(axis)
    return lax.ppermute(array, axis, [(i, (i + by) % count) for i in range(count)])


def normalize(features, head):
    projected = jnp.dot(features, head, preferred_element_type=jnp.float32)
    inverse = lax.rsqrt(jnp.sum(projected * projected, axis=-1, keepdims=True) + epsilon)
    unit = projected * inverse
    return (unit, unit.astype(jnp.bfloat16), inverse)


def unnormalize(unit, inverse, upstream):
    inner = jnp.sum(unit * upstream, axis=-1, keepdims=True)
    return (inverse * (upstream - unit * inner)).astype(jnp.bfloat16)


def across_rows(left, right):
    return lax.dot_general(
        left, right, (((0,), (0,)), ((), ())), preferred_element_type=jnp.float32
    )


def ring_local(
    photo_features,
    wording_features,
    partner_wording_slot,
    photo_projector_weights,
    wording_projector_weights,
    learned_inverse_heat,
    offset_term,
):
    image_rows = photo_features[0]
    text_rows = wording_features[0]
    targets = partner_wording_slot[0]
    row_count = image_rows.shape[0]
    block_count = lax.axis_size("blk")
    position = lax.axis_index("blk")
    img_unit, img_low, img_inv = normalize(image_rows, photo_projector_weights)
    txt_unit, txt_low, txt_inv = normalize(text_rows, wording_projector_weights)
    exponentiated_heat = learned_inverse_heat[0] * criterion_prefactor
    offsets = jnp.arange(row_count, dtype=jnp.int32)
    d_img = jnp.zeros((row_count, txt_low.shape[1]), jnp.float32)
    panel = txt_low
    partial_value = jnp.zeros((row_count, txt_low.shape[1]), jnp.float32)
    for step_index in range(STEPS):
        if step_index > 0:
            panel = from_behind(panel, "blk", 1)
            partial_value = from_behind(partial_value, "blk", 1)
        cosine_agreement_table = lax.dot_general(
            img_low, panel, (((1,), (1,)), ((), ())), preferred_element_type=jnp.float32
        )
        unbounded_pairwise_array = learned_inverse_heat[0] * cosine_agreement_table + offset_term[0]
        columns = (position - step_index) % block_count * row_count + offsets
        diagonal_label = (targets[:, None] == columns[None, :]).astype(jnp.float32)
        submatrix_block_piece = (
            exponentiated_heat * (jax.nn.sigmoid(unbounded_pairwise_array) - diagonal_label)
        ).astype(jnp.bfloat16)
        d_img = d_img + jnp.dot(submatrix_block_piece, panel, preferred_element_type=jnp.float32)
        partial_value = partial_value + across_rows(submatrix_block_piece, img_low)
    d_txt = from_behind(partial_value, "blk", -(STEPS - 1))
    grad_img = across_rows(image_rows, unnormalize(img_unit, img_inv, d_img))
    grad_txt = across_rows(text_rows, unnormalize(txt_unit, txt_inv, d_txt))
    grad_img, grad_txt = lax.psum((grad_img, grad_txt), ("blk", "rep"))
    return (grad_img, grad_txt)


def reduce_kernel(
    n_z, xi0, xi1, xt0, xt1, di0, di1, dt0, dt1, img_ref, txt_ref,
    give, got0, acc, s1, r1, r2, r3, pool, send, recv
):
    rows, cols = img_ref.shape
    chunks, _, width = acc.shape
    panels, _, wide = give.shape
    per = chunks // panels
    half, quarter = rows // 2, rows // 4
    piece = quarter // n_z
    padded = pool.shape[5]
    z, r = lax.axis_index("blk"), lax.axis_index("rep")
    core, x, y = r % 2, (r // 2) % 2, r // 4
    a1 = x + core * (y - x)
    a2 = y + core * (x - y)
    sibling = r + 1 - 2 * core
    p1 = r + (2 + 2 * core) * (1 - 2 * a1)
    p2 = r + (4 - 2 * core) * (1 - 2 * a2)
    turn = [lax.rem(z + d, n_z) for d in range(n_z)]
    back = [lax.rem(z - d + n_z, n_z) for d in range(n_z)]

    barrier = pltpu.get_barrier_semaphore()
    for who in [(z, sibling), (z, p1), (z, p2)] + [(turn[d], r) for d in range(1, n_z)]:
        pl.semaphore_signal(barrier, inc=1, device_id=who, device_id_type=MESH)
    pl.semaphore_wait(barrier, 2 + n_z)

    def copy(src, dst, c, slot, who):
        return pltpu.make_async_remote_copy(
            src_ref=src,
            dst_ref=dst,
            send_sem=send.at[c, slot],
            recv_sem=recv.at[c, slot],
            device_id=who,
            device_id_type=MESH,
        )

    def of(start, size, step):
        return pl.ds(pl.multiple_of(start, step), size)

    keep1 = of(a1 * half, half, 16)
    give1 = of((1 - a1) * half, half, 16)
    base2 = a1 * half + a2 * quarter
    keep2 = of(base2, quarter, 8)
    give2 = of(a1 * half + (1 - a2) * quarter, quarter, 8)
    own2 = of(a2 * quarter, quarter, 16)
    other2 = of((1 - a2) * quarter, quarter, 16)

    def c0(m):
        return copy(give.at[m], got0.at[m], m, 0, (z, sibling))

    def c1(c):
        return copy(s1.at[c], r1.at[c], c, 1, (z, p1))

    def c2(c):
        return copy(acc.at[c, give2], r2.at[c], c, 2, (z, p2))

    def c3(c, d):
        src = acc.at[c, of(base2 + turn[d] * piece, piece, 8)]
        return copy(src, r3.at[c, d], c, 2 + d, (turn[d], r))

    def g3(c, d, at):
        slot = pool.at[c, core, a1, a2, at]
        return copy(slot, slot, c, 1 + n_z + d, (turn[d], r))

    def g2(c, part):
        slot = pool.at[c, core, a1, part]
        return copy(slot, slot, c, 1 + 2 * n_z, (z, p2))

    def g1(c, part):
        slot = pool.at[c, core, part]
        return copy(slot, slot, c, 2 + 2 * n_z, (z, p1))

    def g0(c, part):
        slot = pool.at[c, part]
        return copy(slot, slot, c, 3 + 2 * n_z, (z, sibling))

    tile = rows // 3

    def product(left, right, m, store):
        columns = pl.ds(m * wide, wide)

        def body(i, carry):
            at = pl.ds(pl.multiple_of(i * tile, tile), tile)
            store(
                at,
                across_rows(left[0][:, at], right[0][:, columns])
                + across_rows(left[1][:, at], right[1][:, columns]),
            )
            return carry

        lax.fori_loop(0, rows // tile, body, 0)

    def of_head(head, m, store):
        if head == 0:
            product((xi0, xi1), (di0, di1), m, store)
        else:
            product((xt0, xt1), (dt0, dt1), m, store)

    def theirs(m):
        def store(at, value):
            give[m, at, :] = value

        for mine in range(2):
            @pl.when(core == mine)
            def _():
                of_head(1 - mine, m, store)

        c0(m).start()

    def ours(m):
        def store(at, value):
            for j in range(per):
                acc[m * per + j, at, :] = value[:, j * width : (j + 1) * width]

        for mine in range(2):
            @pl.when(core == mine)
            def _():
                of_head(mine, m, store)

    def stage1(c):
        m, part = c // per, pl.ds(c % per * width, width)
        if c % per == 0:
            c0(m).wait()
        s1[c] = (acc[c, give1, :] + got0[m, give1, part]).astype(s1.dtype)
        c1(c).start()
        acc[c, keep1, :] = acc[c, keep1, :] + got0[m, keep1, part]

    def stage2(c):
        c1(c).wait()
        acc[c, give2, :] = acc[c, give2, :] + r1[c, other2, :].astype(jnp.float32)
        c2(c).start()
        acc[c, keep2, :] = acc[c, keep2, :] + r1[c, own2, :].astype(jnp.float32)

    def stage3(c):
        c2(c).wait()
        acc[c, keep2, :] = acc[c, keep2, :] + r2[c]
        for d in range(1, n_z):
            c3(c, d).start()

    def stage4(c):
        total = acc[c, of(base2 + z * piece, piece, 8), :]
        for d in range(1, n_z):
            c3(c, d).wait()
            total = total + r3[c, d]
        if padded > piece:
            total = jnp.concatenate([total, jnp.zeros((padded - piece, width), jnp.float32)], axis=0)
        pool[c, core, a1, a2, z] = total.astype(pool.dtype)
        for d in range(1, n_z):
            g3(c, d, z).start()

    def stage5(c):
        for d in range(1, n_z):
            g3(c, d, back[d]).wait_recv()
        g2(c, a2).start()

    def stage6(c):
        g2(c, 1 - a2).wait_recv()
        g1(c, a1).start()

    def stage7(c):
        g1(c, 1 - a1).wait_recv()
        g0(c, core).start()

    def stage8(c):
        g0(c, 1 - core).wait_recv()
        for head, ref in ((0, img_ref), (1, txt_ref)):
            for k in range(4 * n_z):
                value = pool[c, head, k // (2 * n_z), k // n_z % 2, k % n_z].astype(jnp.float32)
                ref[k * piece : (k + 1) * piece, c * width : (c + 1) * width] = value[:piece]
        for d in range(1, n_z):
            g3(c, d, z).wait_send()
        g2(c, a2).wait_send()
        g1(c, a1).wait_send()
        g0(c, core).wait_send()

    for m in range(panels):
        theirs(m)
    stages = [stage1, stage2, stage3, stage4, stage5, stage6, stage7, stage8]
    for tick in range(chunks + len(stages) - 1):
        if tick < chunks and tick % per == 0:
            ours(tick // per)
        for at in range(len(stages)):
            if 0 <= tick - at < chunks:
                stages[at](tick - at)


def reduce_all(operands, n_z):
    rows, cols = operands[0].shape[1], operands[4].shape[1]
    half, quarter = rows // 2, rows // 4
    piece = quarter // n_z
    padded = -(-piece // PAD) * PAD
    chunks, width = cols // WIDTH, WIDTH
    panels = chunks // 3
    low, full = jnp.bfloat16, jnp.float32
    return pl.pallas_call(
        functools.partial(reduce_kernel, n_z),
        out_shape=[jax.ShapeDtypeStruct((rows, cols), full)] * 2,
        in_specs=[pl.BlockSpec(memory_space=pltpu.VMEM)] * 8,
        out_specs=[pl.BlockSpec(memory_space=pltpu.VMEM)] * 2,
        scratch_shapes=[
            pltpu.VMEM((panels, rows, 3 * width), full),
            pltpu.VMEM((panels, rows, 3 * width), full),
            pltpu.VMEM((chunks, rows, width), full),
            pltpu.VMEM((chunks, half, width), low),
            pltpu.VMEM((chunks, half, width), low),
            pltpu.VMEM((chunks, quarter, width), full),
            pltpu.VMEM((chunks, n_z, piece, width), full),
            pltpu.VMEM((chunks, 2, 2, 2, n_z, padded, width), low),
            pltpu.SemaphoreType.DMA((chunks, 4 + 2 * n_z)),
            pltpu.SemaphoreType.DMA((chunks, 4 + 2 * n_z)),
        ],
        compiler_params=pltpu.CompilerParams(
            collective_id=0, has_side_effects=True, vmem_limit_bytes=58 * 1024 * 1024
        ),
        cost_estimate=pl.CostEstimate(flops=6 * 10**9, bytes_accessed=10**8, transcendentals=0),
    )(*operands)


def tile_local(
    photo_features,
    wording_features,
    partner_wording_slot,
    photo_projector_weights,
    wording_projector_weights,
    learned_inverse_heat,
    offset_term,
):
    position = lax.axis_index("blk")
    row_count = photo_features.shape[1]
    swap1 = [(i, i ^ 1) for i in range(4)]
    swap2 = [(i, i ^ 2) for i in range(4)]
    photos = [photo_features[0], lax.ppermute(photo_features[0], "blk", swap1)]
    wordings = [wording_features[0], lax.ppermute(wording_features[0], "blk", swap2)]
    targets = [partner_wording_slot[0], lax.ppermute(partner_wording_slot[0], "blk", swap1)]
    text_block = [position, (position + 2) % 4]
    heat, offset = learned_inverse_heat[0], offset_term[0]
    offsets = jnp.arange(row_count, dtype=jnp.int32)
    images = [normalize(rows, photo_projector_weights) for rows in photos]
    texts = [normalize(rows, wording_projector_weights) for rows in wordings]

    def resid(a, b):
        cosine = lax.dot_general(
            images[a][1], texts[b][1], (((1,), (1,)), ((), ())), preferred_element_type=jnp.float32
        )
        label = (targets[a][:, None] == (text_block[b] * row_count + offsets)[None, :]).astype(jnp.float32)
        return (heat * criterion_prefactor * (jax.nn.sigmoid(heat * cosine + offset) - label)).astype(jnp.bfloat16)

    pieces = [[resid(a, b) for b in range(2)] for a in range(2)]

    d_img = [
        sum(jnp.dot(pieces[a][b], texts[b][1], preferred_element_type=jnp.float32) for b in range(2))
        for a in range(2)
    ]
    d_txt = [sum(across_rows(pieces[a][b], images[a][1]) for a in range(2)) for b in range(2)]
    lefts = photos + wordings
    rights = [unnormalize(own[0], own[2], up) for own, up in zip(images + texts, d_img + d_txt)]
    return tuple(reduce_all(lefts + rights, 4))


def solution(mesh):
    placed = (P("rep", "blk", None), P("rep", "blk", None), P("rep", "blk"), P(), P(), P(), P())
    tiled = mesh.shape["blk"] == STEPS == 4 and mesh.shape["rep"] == 8
    body = tile_local if tiled else ring_local
    return jax.shard_map(body, mesh=mesh, in_specs=placed, out_specs=(P(), P()), check_vma=False)
```
